256 devices in a mesh: row: 8 (over y, core), col: 32 (over z, x).
Axes of the slice: x: 4, y: 4, z: 8, core: 2. Of those that a mesh axis runs over, the one named last changes fastest.
Arguments:
- momentum: float32 [8192, 14336], P('row', 'col'), may hold values from -12 to 12
- gradient: float32 [8192, 14336], P('row', 'col'), may hold values from -6 to 6
- right_factor: float32 [14336, 256], P('col'), may hold values from -0.046875 to 0.046875
Outputs:
- momentum_next: float32 [8192, 14336], P('row', 'col')
- update: float32 [8192, 14336], P('row', 'col')
The draws below stay inside these ranges and needn't reach their ends.
All inputs are finite; a program needn't handle non-finite values.
Results may differ from the reference program's by a relative error of at most 0.002.
Values sent between devices are 32-bit elements; how exact they have to be, the bound alone decides.
No kernel may reach another device: no remote copies, remote signals or barrier semaphores. Data moves between devices by JAX's collectives and lax.ppermute only.
A program may use at most 64 MiB of HBM per device.

```python
import jax
import jax.numpy as jnp
from jax import lax

D = 8192
FF = 14336
RANK = 256
ITERS = 2


def block_levels(rng, extent, cuts, smallest, high):
    def one(position, blocks):
        steps = jax.random.uniform(jax.random.fold_in(jax.random.fold_in(rng, 6), position), (blocks,), jnp.float32, smallest / len(cuts), high / len(cuts))
        return jnp.repeat(jnp.exp(steps), extent[position] // blocks).reshape((-1,) + (1,) * (len(extent) - position - 1))

    gain = one(*cuts[0])
    for cut in cuts[1:]:
        gain = gain * one(*cut)
    return gain


def scatter_about(stream_key, dims, width, reach, pieces=(), kind=jnp.bfloat16):
    values = width * jax.random.normal(stream_key, dims, jnp.float32)
    if pieces:
        values = values * block_levels(stream_key, dims, pieces, -0.22, 0.18)
    return jnp.clip(values, -reach, reach).astype(kind)


def setup_inputs(seed: int = 0) -> dict:
    splits = jax.random.split(jax.random.key(seed), 4)
    return {
        "momentum": scatter_about(splits[0], (D, FF), 2.0, 12.0, ((0, 8), (1, 32)), jnp.float32),
        "gradient": scatter_about(splits[1], (D, FF), 1.0, 6.0, ((0, 8), (1, 32)), jnp.float32),
        "right_factor": scatter_about(splits[2], (FF, RANK), FF ** -0.5, 0.046875, ((0, 32),), jnp.float32),
    }


MU = 0.95

def orthonormal(left):
    gram = jnp.dot(left.T, left, precision=lax.Precision.HIGHEST)
    lower = jnp.linalg.cholesky(gram)
    return lax.linalg.triangular_solve(lower, left, left_side=False, lower=True, transpose_a=True)

def reference(momentum, gradient, right_factor):
    buffer = momentum + gradient
    right = right_factor
    left = None
    carried = None
    for step in range(ITERS):
        left = jnp.dot(buffer, right, precision=lax.Precision.HIGHEST)
        left = orthonormal(left)
        carried = jnp.dot(buffer.T, left, precision=lax.Precision.HIGHEST)
        norms = jnp.sqrt(lax.optimization_barrier(jnp.sum(carried * carried, axis=0)) + 1e-06)
        right = carried / norms
    momentum_next = buffer - (1.0 - MU) * jnp.dot(left, carried.T, precision=lax.Precision.HIGHEST)
    factor = jnp.float32((D * FF / RANK) ** 0.5)
    update = factor * jnp.dot(left, right.T, precision=lax.Precision.HIGHEST)
    return (momentum_next, update)
```

```python
import jax
import jax.numpy as jnp
from jax import lax
from jax.experimental import pallas as pl
from jax.sharding import PartitionSpec as P

D = 8192
FF = 14336
RANK = 256
MU = 0.95
EPS = 1e-06

HIGH = lax.Precision.HIGH
HIGHEST = lax.Precision.HIGHEST

X_GROUPS = [[z * 4 + x for x in range(4)] for z in range(8)]
Z_GROUPS = [[z * 4 + x for z in range(8)] for x in range(4)]
Y_GROUPS = [[y * 2 + c for y in range(4)] for c in range(2)]
OTHER_CORE = [(i, i ^ 1) for i in range(8)]


def dot(a, b, contract, precision):
    return lax.dot_general(
        a, b, (contract, ((), ())), precision=precision, preferred_element_type=jnp.float32
    )


def factor(block):
    size = block.shape[0]
    count = size // 8
    groups = [block[8 * g : 8 * g + 8, :] for g in range(count)]
    lane = lax.broadcasted_iota(jnp.int32, (8, size), 1)
    sub = lax.broadcasted_iota(jnp.int32, (8, size), 0)
    for j in range(size):
        first, r = divmod(j, 8)
        here = lane == j
        row = jnp.broadcast_to(groups[first][r : r + 1, :], (8, size))
        inverse = 1.0 / jnp.broadcast_to(row[:, j : j + 1], (8, size))
        scaled = jnp.where(here, 1.0, row) * inverse
        for g in range(first, count):
            old = groups[g]
            multiplier = jnp.broadcast_to(old[:, j : j + 1], (8, size))
            new = jnp.where(here, 0.0, old) - multiplier * scaled
            groups[g] = jnp.where(sub > r, new, old) if g == first else new
    rows = []
    for g in range(count):
        row = sub + 8 * g
        pivot = jnp.sum(jnp.where(lane == row, groups[g], 0.0), axis=1, keepdims=True)
        unit = jnp.where(lane < row, groups[g], jnp.where(lane == row, 1.0, 0.0))
        rows.append(unit * lax.rsqrt(pivot))
    return jnp.concatenate(rows, 0)


def cholesky_inverse_kernel(gram_ref, out_ref):
    h = RANK // 2
    top = factor(gram_ref[0:h, 0:h])
    lower = dot(gram_ref[h:, 0:h], top, ((1,), (1,)), HIGHEST)
    bottom = factor(gram_ref[h:, h:] - dot(lower, lower, ((1,), (1,)), HIGHEST))
    corner = dot(bottom, dot(lower, top, ((1,), (0,)), HIGHEST), ((1,), (0,)), HIGHEST)
    out_ref[0:h, 0:h] = top
    out_ref[0:h, h:] = jnp.zeros((h, h), jnp.float32)
    out_ref[h:, 0:h] = -corner
    out_ref[h:, h:] = bottom


def cholesky_inverse(gram):
    return pl.pallas_call(
        cholesky_inverse_kernel, out_shape=jax.ShapeDtypeStruct((RANK, RANK), jnp.float32)
    )(gram)


def scatter_sum(value, axis, groups):
    n = len(groups[0])
    value = lax.all_to_all(value, axis, 0, 0, tiled=True, axis_index_groups=groups)
    return jnp.sum(value.reshape(n, -1, RANK), axis=0)


def gather(value, axis, groups):
    n = len(groups[0])
    value = jnp.tile(value, (n, 1))
    return lax.all_to_all(value, axis, 0, 0, tiled=True, axis_index_groups=groups)


def sum_over_col(value):
    with jax.named_scope("sum_over_col"):
        value = scatter_sum(value, "col", X_GROUPS)
        value = scatter_sum(value, "col", Z_GROUPS)
        value = gather(value, "col", Z_GROUPS)
        return gather(value, "col", X_GROUPS)


def sum_over_row(value):
    with jax.named_scope("sum_over_row"):
        half = value.shape[0] // 2
        core = lax.axis_index("row") % 2
        mine = lax.dynamic_slice_in_dim(value, core * half, half)
        theirs = lax.dynamic_slice_in_dim(value, (1 - core) * half, half)
        value = mine + lax.ppermute(theirs, "row", OTHER_CORE)
        value = scatter_sum(value, "row", Y_GROUPS)
        value = gather(value, "row", Y_GROUPS)
        other = lax.ppermute(value, "row", OTHER_CORE)
        first = jnp.where(core == 0, value, other)
        second = jnp.where(core == 0, other, value)
        return jnp.concatenate([first, second], 0)


def on_device(momentum, gradient, right_factor):
    cols = momentum.shape[1]
    buffer = momentum + gradient
    left = sum_over_col(dot(buffer, right_factor, ((1,), (0,)), HIGH))
    carried = dot(buffer, left, ((0,), (0,)), HIGH)
    gram = dot(left, left, ((0,), (0,)), HIGHEST)
    both = sum_over_row(jnp.concatenate([carried, gram], 0))
    carried, gram = both[:cols], both[cols:]
    inverse = cholesky_inverse(gram)
    carried = dot(carried, inverse, ((1,), (1,)), HIGHEST)
    left = dot(left, inverse, ((1,), (1,)), HIGHEST)
    product = sum_over_col(dot(buffer, carried, ((1,), (0,)), HIGH))
    squares = jnp.sum(left * product, axis=0, keepdims=True)
    carried = dot(buffer, product, ((0,), (0,)), HIGH)
    gram = dot(product, product, ((0,), (0,)), HIGHEST)
    both = sum_over_row(
        jnp.concatenate([carried, gram, jnp.pad(squares, ((0, 63), (0, 0)))], 0)
    )
    carried, gram, squares = both[:cols], both[cols : cols + RANK], both[cols + RANK]
    scale = 1.0 / jnp.sqrt(jnp.maximum(squares, 0.0) + EPS)
    inverse = cholesky_inverse(gram * scale[:, None] * scale[None, :]) * scale[None, :]
    left = dot(product, inverse, ((1,), (1,)), HIGHEST)
    carried = dot(carried, inverse, ((1,), (1,)), HIGHEST)
    squares = jnp.sum(carried * carried, axis=0, keepdims=True)
    squares = lax.all_to_all(jnp.tile(squares, (32, 1)), "col", 0, 0, tiled=True)
    squares = jnp.sum(squares, axis=0, keepdims=True)
    factor_ = jnp.float32((D * FF / RANK) ** 0.5)
    right = carried * (factor_ / jnp.sqrt(squares + EPS))
    momentum_next = buffer - (1.0 - MU) * dot(left, carried, ((1,), (1,)), HIGH)
    update = dot(left, right, ((1,), (1,)), HIGH)
    return (momentum_next, update)


def solution(mesh):
    return jax.shard_map(
        on_device,
        mesh=mesh,
        in_specs=(P("row", "col"), P("row", "col"), P("col", None)),
        out_specs=(P("row", "col"), P("row", "col")),
        check_vma=False,
    )
```

```python
import functools

import jax
import jax.numpy as jnp
from jax import lax
from jax.experimental import pallas as pl
from jax.experimental.pallas import tpu as pltpu
from jax.sharding import PartitionSpec as P

D = 8192
FF = 14336
RANK = 256
MU = 0.95
EPS = 1e-06
ROWS = 1024
COLS = 448
BLOCK = ROWS // 4
FIRST = COLS + RANK
GRAM = RANK + 16
PART = COLS // 8

HIGHEST = lax.Precision.HIGHEST
LIMIT = 24 * 1024 * 1024

X_SHIFTS = [[(i, i // 4 * 4 + (i + k) % 4) for i in range(32)] for k in (1, 2, 3)]
Z_GROUPS = [[z * 4 + x for z in range(8)] for x in range(4)]
Y_GROUPS = [[y * 2 + c for y in range(4)] for c in range(2)]
Y_SHIFTS = [[(i, (i // 2 + k) % 4 * 2 + i % 2) for i in range(8)] for k in (1, 2, 3)]
OTHER_CORE = [(i, i ^ 1) for i in range(8)]

VMEM = pl.BlockSpec(memory_space=pltpu.VMEM)
SMEM = pl.BlockSpec(memory_space=pltpu.SMEM)
HBM = pl.BlockSpec(memory_space=pltpu.HBM)


def shape(*dims):
    return jax.ShapeDtypeStruct(dims, jnp.float32)


def scratch(*dims):
    return pltpu.VMEM(dims, jnp.float32)


def params(**more):
    return pltpu.CompilerParams(vmem_limit_bytes=LIMIT, **more)


def cost(flops):
    return pl.CostEstimate(flops=flops, bytes_accessed=1_000_000, transcendentals=0)


def dot(a, b, contract, precision=HIGHEST):
    return lax.dot_general(
        a, b, (contract, ((), ())), precision=precision, preferred_element_type=jnp.float32
    )


def split(value):
    high = value.astype(jnp.bfloat16)
    return high, (value - high.astype(jnp.float32)).astype(jnp.bfloat16)


def dot3(a, b, contract):
    (a0, a1), (b0, b1) = a, b
    one = functools.partial(dot, contract=contract, precision=None)
    return one(a0, b0) + (one(a0, b1) + one(a1, b0))


def full(value, size):
    return jnp.broadcast_to(value, (8, size))


def factor(block):
    size = block.shape[0]
    count = size // 8
    groups = [block[8 * g : 8 * g + 8, :] for g in range(count)]
    lane = lax.broadcasted_iota(jnp.int32, (8, size), 1)
    sub = lax.broadcasted_iota(jnp.int32, (8, size), 0)
    pivots = []
    for p in range(count):
        base = 8 * p
        own = groups[p]
        rows = [full(own[k : k + 1, :], size) for k in range(8)]
        columns = [full(own[:, base + i : base + i + 1], size) for i in range(8)]
        s = [[full(columns[i][k : k + 1, :], size) for i in range(k + 1)] for k in range(8)]
        inverse = [None] * 8
        low = [[None] * 8 for _ in range(8)]
        for j in range(0, 8, 2):
            a, b, c = s[j][j], s[j + 1][j], s[j + 1][j + 1]
            det = a * c - b * b
            inverse_det = 1.0 / det
            inverse[j] = 1.0 / a
            inverse[j + 1] = a * inverse_det
            low[j + 1][j] = b * inverse[j]
            before = {k: (s[k][j], s[k][j + 1]) for k in range(j + 2, 8)}
            for k in range(j + 2, 8):
                u, v = before[k]
                w0 = (c * u - b * v) * inverse_det
                w1 = (a * v - b * u) * inverse_det
                for i in range(j + 2, k + 1):
                    s[k][i] = s[k][i] - (w0 * before[i][0] + w1 * before[i][1])
                low[k][j] = u * inverse[j]
                low[k][j + 1] = w1
                s[k][j + 1] = v - low[k][j] * b
            s[j + 1][j + 1] = det * inverse[j]
        for j in range(8):
            here = lane == base + j
            row = jnp.where(here, 1.0, rows[j])
            for k in range(j + 1, 8):
                rows[k] = jnp.where(here, 0.0, rows[k]) - low[k][j] * row
        inside = (lane >= base) & (lane < base + 8)
        tails = [
            jnp.where(inside & (lane > base + j), 0.0, jnp.where(lane == base + j, 1.0, rows[j]))
            for j in range(8)
        ]
        for g in range(p + 1, count):
            old = groups[g]
            values = [full(old[:, base + i : base + i + 1], size) for i in range(8)]
            terms = []
            for j in range(8):
                multiplier = values[j] * inverse[j]
                for i in range(j + 1, 8):
                    values[i] = values[i] - multiplier * s[i][j]
                terms.append(multiplier * tails[j])
            while len(terms) > 1:
                terms = [terms[i] + terms[i + 1] for i in range(0, len(terms), 2)]
            groups[g] = jnp.where(inside, 0.0, old) - terms[0]
        merged, pivot = rows[0], s[0][0]
        for k in range(1, 8):
            merged = jnp.where(sub == k, rows[k], merged)
            pivot = jnp.where(sub == k, s[k][k], pivot)
        groups[p] = merged
        pivots.append(pivot)
    out = []
    for g in range(count):
        row = sub + 8 * g
        unit = jnp.where(lane < row, groups[g], jnp.where(lane == row, 1.0, 0.0))
        out.append(unit * lax.rsqrt(pivots[g]))
    return jnp.concatenate(out, 0)


def tile_of(position):
    return pl.ds(pl.multiple_of(position * BLOCK, BLOCK), BLOCK)


def half_of(position, size):
    return pl.ds(pl.multiple_of(position * size, 8), size)


def forward_blocks(x, buffer_ref, factor, out_refs):
    factor = split(factor)
    for k in range(4):
        tile = split(buffer_ref[:, tile_of(lax.rem(x + k, 4))])
        out_refs[k][...] = dot3(tile, factor, ((0,), (0,)))


def start_kernel(x_ref, buffer_ref, right_ref, *out_refs):
    forward_blocks(x_ref[0], buffer_ref, right_ref[...], out_refs)


def start(x, buffer, right):
    return pl.pallas_call(
        start_kernel,
        in_specs=[SMEM, VMEM, VMEM],
        out_specs=[VMEM] * 4,
        out_shape=[shape(BLOCK, RANK)] * 4,
        compiler_params=params(),
        name="start",
    )(x, buffer, right)


def forward_kernel(x_ref, core_ref, buffer_ref, half_ref, other_ref, *rest):
    *out_refs, gram_ref, both = rest
    core = core_ref[0]
    both[half_of(core, FIRST // 2), :] = half_ref[...]
    both[half_of(1 - core, FIRST // 2), :] = other_ref[...]
    gram_ref[...] = both[COLS:FIRST, :]
    forward_blocks(x_ref[0], buffer_ref, both[0:COLS, :], out_refs)


def forward(x, core, buffer, half, other):
    return pl.pallas_call(
        forward_kernel,
        in_specs=[SMEM, SMEM, VMEM, VMEM, VMEM],
        out_specs=[VMEM] * 5,
        out_shape=[shape(BLOCK, RANK)] * 5,
        scratch_shapes=[scratch(FIRST, RANK)],
        compiler_params=params(),
        name="forward",
    )(x, core, buffer, half, other)


def backward_kernel(x_ref, core_ref, buffer_ref, *rest):
    *left_refs, mine_ref, theirs_ref, left, both = rest
    x, core = x_ref[0], core_ref[0]
    for k in range(4):
        left[tile_of(lax.rem(x + 4 - k, 4)), :] = left_refs[k][...]
    both[0:COLS, :] = dot3(split(buffer_ref[...]), split(left[...]), ((1,), (0,)))
    both[COLS:FIRST, :] = dot(left[...], left[...], ((0,), (0,)))
    mine_ref[...] = both[half_of(core, FIRST // 2), :]
    theirs_ref[...] = both[half_of(1 - core, FIRST // 2), :]


def backward(x, core, buffer, left):
    return pl.pallas_call(
        backward_kernel,
        in_specs=[SMEM, SMEM] + [VMEM] * 5,
        out_specs=[VMEM] * 2,
        out_shape=[shape(FIRST // 2, RANK)] * 2,
        scratch_shapes=[scratch(ROWS, RANK), scratch(FIRST, RANK)],
        compiler_params=params(),
        name="backward",
    )(x, core, buffer, *left)


def prepare_kernel(x_ref, inverse_ref, *rest):
    *left_refs, old_ref = rest
    x = x_ref[0]
    inverse = split(inverse_ref[...])
    for k in range(4):
        place = tile_of(lax.rem(x + 4 - k, 4))
        old_ref[place, :] = dot3(split(left_refs[k][...]), inverse, ((1,), (1,)))


def prepare(x, inverse, left):
    return pl.pallas_call(
        prepare_kernel,
        in_specs=[SMEM] + [VMEM] * 5,
        out_specs=VMEM,
        out_shape=shape(ROWS, RANK),
        cost_estimate=cost(2_000_000_000),
        compiler_params=params(),
        name="prepare",
    )(x, inverse, *left)


def solve_kernel(x_ref, core_ref, buffer_ref, inverse_ref, old_ref, *rest):
    product_refs = rest[0:4]
    mine_ref, theirs_ref, out_ref, carried, gram = rest[4:]
    x, core = x_ref[0], core_ref[0]
    for k in range(4):
        place = tile_of(lax.rem(x + 4 - k, 4))
        out_ref[place, :] = dot(product_refs[k][...], inverse_ref[...], ((1,), (1,)))
    product = out_ref[...]
    carried[...] = dot3(split(buffer_ref[...]), split(product), ((1,), (0,)))
    gram[0:RANK, :] = dot(product, product, ((0,), (0,)))
    gram[RANK:GRAM, :] = jnp.zeros((GRAM - RANK, RANK), jnp.float32)
    gram[RANK : RANK + 1, :] = jnp.sum(old_ref[...] * product, axis=0, keepdims=True)
    for half_ref, position in ((mine_ref, core), (theirs_ref, 1 - core)):
        half_ref[0 : GRAM // 2, :] = gram[half_of(position, GRAM // 2), :]
        half_ref[GRAM // 2 :, :] = carried[half_of(position, COLS // 2), :]


def solve(x, core, buffer, inverse, old, product):
    return pl.pallas_call(
        solve_kernel,
        in_specs=[SMEM, SMEM] + [VMEM] * 7,
        out_specs=[VMEM] * 3,
        out_shape=[shape(GRAM // 2 + COLS // 2, RANK)] * 2 + [shape(ROWS, RANK)],
        scratch_shapes=[scratch(COLS, RANK), scratch(GRAM, RANK)],
        compiler_params=params(),
        name="solve",
    )(x, core, buffer, inverse, old, *product)


def cholesky_inverse(gram_ref, out_ref, block, corner):
    h = RANK // 2
    block[...] = gram_ref[0:h, 0:h]

    def step(k, _):
        inverse = factor(block[...])
        out_ref[half_of(k, h), 0:h] = inverse

        @pl.when(k == 0)
        def _():
            lower = dot(gram_ref[h:, 0:h], inverse, ((1,), (1,)))
            block[...] = gram_ref[h:, h:] - dot(lower, lower, ((1,), (1,)))
            corner[...] = dot(lower, inverse, ((1,), (0,)))

        return 0

    lax.fori_loop(0, 2, step, 0)
    bottom = out_ref[h:, 0:h]
    out_ref[h:, 0:h] = -dot(bottom, corner[...], ((1,), (0,)))
    out_ref[h:, h:] = bottom
    out_ref[0:h, h:] = jnp.zeros((h, h), jnp.float32)


def first_inverse(gram):
    return pl.pallas_call(
        cholesky_inverse,
        in_specs=[VMEM],
        out_specs=VMEM,
        out_shape=shape(RANK, RANK),
        scratch_shapes=[scratch(RANK // 2, RANK // 2)] * 2,
        cost_estimate=cost(10_000_000_000),
        compiler_params=params(),
        name="first_inverse",
    )(gram)


def second_kernel(core_ref, half_ref, other_ref, out_ref, whole, gram, inverse, block, corner):
    core = core_ref[0]
    whole[half_of(core, GRAM // 2), :] = half_ref[0 : GRAM // 2, :]
    whole[half_of(1 - core, GRAM // 2), :] = other_ref[0 : GRAM // 2, :]
    scale = 1.0 / jnp.sqrt(jnp.maximum(whole[RANK : RANK + 1, :], 0.0) + EPS)
    gram[...] = (whole[0:RANK, :] * scale).T * scale
    cholesky_inverse(gram, inverse, block, corner)
    h, q = RANK // 2, RANK // 4
    out_ref[0:h, :] = inverse[h:, :] * scale
    out_ref[h:, 0:h] = inverse[0:q, 0:h] * scale[:, 0:h]
    out_ref[h:, h:] = inverse[q:h, 0:h] * scale[:, 0:h]


def times_inverse(value, packed):
    h = RANK // 2
    top = jnp.concatenate([packed[h:, 0:h], packed[h:, h:]], 0)
    left = dot(value[:, 0:h], top, ((1,), (1,)))
    return jnp.concatenate([left, dot(value, packed[0:h, :], ((1,), (1,)))], 1)


def second_inverse(core, half, other):
    return pl.pallas_call(
        second_kernel,
        in_specs=[SMEM, VMEM, VMEM],
        out_specs=VMEM,
        out_shape=shape(RANK * 3 // 4, RANK),
        scratch_shapes=[scratch(GRAM, RANK), scratch(RANK, RANK), scratch(RANK, RANK)]
        + [scratch(RANK // 2, RANK // 2)] * 2,
        cost_estimate=cost(10_000_000_000),
        compiler_params=params(),
        name="second_inverse",
    )(core, half, other)


def finish_kernel(core_ref, y_ref, inverse_ref, *rest):
    *part_refs, carried_ref, squares_ref, whole = rest
    core, y = core_ref[0], y_ref[0]
    for k in range(4):
        place = lax.rem(y + 4 - k, 4)
        whole[half_of(4 * core + place, PART), :] = part_refs[k][0:PART, :]
        whole[half_of(4 * (1 - core) + place, PART), :] = part_refs[k][PART : 2 * PART, :]
    carried = times_inverse(whole[...], inverse_ref[...])
    carried_ref[...] = carried
    squares = jnp.sum(carried * carried, axis=0, keepdims=True)
    for k in range(32):
        squares_ref[k] = squares


def finish(core, y, inverse, parts):
    return pl.pallas_call(
        finish_kernel,
        in_specs=[SMEM, SMEM] + [VMEM] * 5,
        out_specs=[VMEM] * 2,
        out_shape=[shape(COLS, RANK), shape(32, 1, RANK)],
        scratch_shapes=[scratch(COLS, RANK)],
        compiler_params=params(),
        name="finish",
    )(core, y, inverse, *parts)


def send_columns(out_hbm, staged, semaphores, give):
    wide = ROWS // 2

    def copy(k):
        place = pl.ds(pl.multiple_of(k * wide, wide), wide)
        return pltpu.make_async_copy(staged.at[k], out_hbm.at[:, place], semaphores.at[k])

    def step(k, _):
        staged[k] = give(pl.ds(pl.multiple_of(k * wide, wide), wide))
        copy(k).start()
        return 0

    lax.fori_loop(0, 2, step, 0)
    for k in range(2):
        copy(k).wait()


def feedback_kernel(
    buffer_ref, product_ref, inverse_ref, carried_ref, out_hbm, left_ref, *rest
):
    left_ref[...] = times_inverse(product_ref[...], inverse_ref[...])
    carried = split(carried_ref[...])

    def give(place):
        change = dot3(carried, split(left_ref[place, :]), ((1,), (1,)))
        return buffer_ref[:, place] - (1.0 - MU) * change

    send_columns(out_hbm, *rest, give)


def feedback(buffer, product, inverse, carried):
    return pl.pallas_call(
        feedback_kernel,
        in_specs=[VMEM] * 4,
        out_specs=[HBM, VMEM],
        out_shape=[shape(COLS, ROWS), shape(ROWS, RANK)],
        input_output_aliases={1: 1},
        scratch_shapes=[scratch(2, COLS, ROWS // 2), pltpu.SemaphoreType.DMA((2,))],
        cost_estimate=cost(4_000_000_000),
        compiler_params=params(),
        name="feedback",
    )(buffer, product, inverse, carried)


def update_kernel(left_ref, carried_ref, squares_ref, out_hbm, *rest):
    squares = squares_ref[0]
    for k in range(1, 32):
        squares = squares + squares_ref[k]
    right = carried_ref[...] * (((D * FF / RANK) ** 0.5) / jnp.sqrt(squares + EPS))
    right = split(right)

    def give(place):
        return dot3(right, split(left_ref[place, :]), ((1,), (1,)))

    send_columns(out_hbm, *rest, give)


def update(left, carried, squares):
    return pl.pallas_call(
        update_kernel,
        in_specs=[VMEM] * 3,
        out_specs=HBM,
        out_shape=shape(COLS, ROWS),
        scratch_shapes=[scratch(2, COLS, ROWS // 2), pltpu.SemaphoreType.DMA((2,))],
        compiler_params=params(),
        name="update",
    )(left, carried, squares)


def fold_kernel(parts, value_ref, out_ref):
    size = out_ref.shape[0] // parts
    total = value_ref[0:size, :]
    for k in range(1, parts):
        total = total + value_ref[k * size : (k + 1) * size, :]
    for k in range(parts):
        out_ref[k * size : (k + 1) * size, :] = total


def sum_by_exchange(value, axis, groups):
    value = lax.all_to_all(value, axis, 0, 0, tiled=True, axis_index_groups=groups)
    value = pl.pallas_call(
        functools.partial(fold_kernel, len(groups[0])),
        in_specs=[VMEM],
        out_specs=VMEM,
        out_shape=shape(*value.shape),
        compiler_params=params(),
        name="fold",
    )(value)
    return lax.all_to_all(value, axis, 0, 0, tiled=True, axis_index_groups=groups)


def sum_over_col(blocks, beside):
    with jax.named_scope("sum_over_col"):
        total = blocks[0]
        for k in (3, 2, 1):
            total = total + lax.ppermute(blocks[k], "col", X_SHIFTS[k - 1])
        total, beside = lax.optimization_barrier((total, beside))
        total = sum_by_exchange(total, "col", Z_GROUPS)
        rest = [lax.ppermute(total, "col", X_SHIFTS[k - 1]) for k in (1, 2, 3)]
        return [total] + rest, beside


def sum_over_row(mine, theirs):
    with jax.named_scope("sum_over_row"):
        half = mine + lax.ppermute(theirs, "row", OTHER_CORE)
        half = sum_by_exchange(half, "row", Y_GROUPS)
        return half, lax.ppermute(half, "row", OTHER_CORE)


def sum_and_invert(core, y, mine, theirs):
    with jax.named_scope("sum_and_invert"):
        half = mine + lax.ppermute(theirs, "row", OTHER_CORE)
        gram, half = half[: GRAM // 2], half[GRAM // 2 :]

        def share(k):
            part = lax.dynamic_slice_in_dim(half, (y[0] + k) % 4 * PART, PART)
            return jnp.concatenate([gram, part], 0)

        total = share(0)
        for k in (1, 2, 3):
            total = total + lax.ppermute(share(k), "row", Y_SHIFTS[k - 1])
        other = lax.ppermute(total, "row", OTHER_CORE)
        inverse = second_inverse(core, total, other)
        part = jnp.concatenate([total[GRAM // 2 :], other[GRAM // 2 :]], 0)
        parts = [part] + [lax.ppermute(part, "row", shift) for shift in Y_SHIFTS]
        return inverse, *finish(core, y, inverse, parts)


def on_device(momentum, gradient, right_factor):
    x = lax.axis_index("col")[None] % 4
    core = lax.axis_index("row")[None] % 2
    y = lax.axis_index("row")[None] // 2
    buffer = momentum.T + gradient.T
    left, buffer = sum_over_col(start(x, buffer, right_factor), buffer)
    half, other = sum_over_row(*backward(x, core, buffer, left))
    *blocks, gram = forward(x, core, buffer, half, other)
    product, inverse = sum_over_col(blocks, first_inverse(gram))
    old = prepare(x, inverse, left)
    mine, theirs, product = solve(x, core, buffer, inverse, old, product)
    inverse, carried, squares = sum_and_invert(core, y, mine, theirs)
    squares = lax.all_to_all(squares, "col", 0, 0, tiled=True)
    momentum_next, left = feedback(buffer, product, inverse, carried)
    return (momentum_next.T, update(left, carried, squares).T)


def solution(mesh):
    return jax.shard_map(
        on_device,
        mesh=mesh,
        in_specs=(P("row", "col"), P("row", "col"), P("col", None)),
        out_specs=(P("row", "col"), P("row", "col")),
        check_vma=False,
    )
```

```python
import functools

import jax
import jax.numpy as jnp
from jax import lax
from jax.experimental import pallas as pl
from jax.experimental.pallas import tpu as pltpu
from jax.sharding import PartitionSpec as P

D = 8192
FF = 14336
RANK = 256
MU = 0.95
EPS = 1e-06
ROWS = 1024
COLS = 448
BLOCK = ROWS // 4
FIRST = COLS + RANK
GRAM = RANK + 16
PART = COLS // 8

HIGHEST = lax.Precision.HIGHEST
LIMIT = 24 * 1024 * 1024

X_SHIFTS = [[(i, i // 4 * 4 + (i + k) % 4) for i in range(32)] for k in (1, 2, 3)]
Z_GROUPS = [[z * 4 + x for z in range(8)] for x in range(4)]
Y_GROUPS = [[y * 2 + c for y in range(4)] for c in range(2)]
Y_SHIFTS = [[(i, (i // 2 + k) % 4 * 2 + i % 2) for i in range(8)] for k in (1, 2, 3)]
OTHER_CORE = [(i, i ^ 1) for i in range(8)]

VMEM = pl.BlockSpec(memory_space=pltpu.VMEM)
SMEM = pl.BlockSpec(memory_space=pltpu.SMEM)
HBM = pl.BlockSpec(memory_space=pltpu.HBM)


def shape(*dims):
    return jax.ShapeDtypeStruct(dims, jnp.float32)


def half_shape(*dims):
    return jax.ShapeDtypeStruct(dims, jnp.bfloat16)


def scratch(*dims):
    return pltpu.VMEM(dims, jnp.float32)


def params(**more):
    return pltpu.CompilerParams(vmem_limit_bytes=LIMIT, **more)


def cost(flops):
    return pl.CostEstimate(flops=flops, bytes_accessed=1_000_000, transcendentals=0)


def dot(a, b, contract, precision=HIGHEST):
    return lax.dot_general(
        a, b, (contract, ((), ())), precision=precision, preferred_element_type=jnp.float32
    )


def split(value):
    high = value.astype(jnp.bfloat16)
    return high, (value - high.astype(jnp.float32)).astype(jnp.bfloat16)


def dot3(a, b, contract):
    (a0, a1), (b0, b1) = a, b
    one = functools.partial(dot, contract=contract, precision=None)
    return one(a0, b0) + (one(a0, b1) + one(a1, b0))


def full(value, size):
    return jnp.broadcast_to(value, (8, size))


def factor(block):
    size = block.shape[0]
    count = size // 8
    groups = [block[8 * g : 8 * g + 8, :] for g in range(count)]
    lane = lax.broadcasted_iota(jnp.int32, (8, size), 1)
    sub = lax.broadcasted_iota(jnp.int32, (8, size), 0)
    pivots = []
    for p in range(count):
        base = 8 * p
        own = groups[p]
        rows = [full(own[k : k + 1, :], size) for k in range(8)]
        columns = [full(own[:, base + i : base + i + 1], size) for i in range(8)]
        s = [[full(columns[i][k : k + 1, :], size) for i in range(k + 1)] for k in range(8)]
        inverse = [None] * 8
        low = [[None] * 8 for _ in range(8)]
        for j in range(0, 8, 2):
            a, b, c = s[j][j], s[j + 1][j], s[j + 1][j + 1]
            det = a * c - b * b
            inverse_det = 1.0 / det
            inverse[j] = 1.0 / a
            inverse[j + 1] = a * inverse_det
            low[j + 1][j] = b * inverse[j]
            before = {k: (s[k][j], s[k][j + 1]) for k in range(j + 2, 8)}
            for k in range(j + 2, 8):
                u, v = before[k]
                w0 = (c * u - b * v) * inverse_det
                w1 = (a * v - b * u) * inverse_det
                for i in range(j + 2, k + 1):
                    s[k][i] = s[k][i] - (w0 * before[i][0] + w1 * before[i][1])
                low[k][j] = u * inverse[j]
                low[k][j + 1] = w1
                s[k][j + 1] = v - low[k][j] * b
            s[j + 1][j + 1] = det * inverse[j]
        for j in range(8):
            here = lane == base + j
            row = jnp.where(here, 1.0, rows[j])
            for k in range(j + 1, 8):
                rows[k] = jnp.where(here, 0.0, rows[k]) - low[k][j] * row
        inside = (lane >= base) & (lane < base + 8)
        tails = [
            jnp.where(inside & (lane > base + j), 0.0, jnp.where(lane == base + j, 1.0, rows[j]))
            for j in range(8)
        ]
        for g in range(p + 1, count):
            old = groups[g]
            values = [full(old[:, base + i : base + i + 1], size) for i in range(8)]
            terms = []
            for j in range(8):
                multiplier = values[j] * inverse[j]
                for i in range(j + 1, 8):
                    values[i] = values[i] - multiplier * s[i][j]
                terms.append(multiplier * tails[j])
            while len(terms) > 1:
                terms = [terms[i] + terms[i + 1] for i in range(0, len(terms), 2)]
            groups[g] = jnp.where(inside, 0.0, old) - terms[0]
        merged, pivot = rows[0], s[0][0]
        for k in range(1, 8):
            merged = jnp.where(sub == k, rows[k], merged)
            pivot = jnp.where(sub == k, s[k][k], pivot)
        groups[p] = merged
        pivots.append(pivot)
    out = []
    for g in range(count):
        row = sub + 8 * g
        unit = jnp.where(lane < row, groups[g], jnp.where(lane == row, 1.0, 0.0))
        out.append(unit * lax.rsqrt(pivots[g]))
    return jnp.concatenate(out, 0)


def tile_of(position):
    return pl.ds(pl.multiple_of(position * BLOCK, BLOCK), BLOCK)


def half_of(position, size):
    return pl.ds(pl.multiple_of(position * size, 8), size)


def forward_blocks(x, buffer_ref, factor, out_refs):
    factor = split(factor)
    for k in range(4):
        tile = split(buffer_ref[:, tile_of(lax.rem(x + k, 4))])
        out_refs[k][...] = dot3(tile, factor, ((0,), (0,)))


def start_kernel(x_ref, buffer_ref, right_ref, *out_refs):
    forward_blocks(x_ref[0], buffer_ref, right_ref[...], out_refs)


def start(x, buffer, right):
    return pl.pallas_call(
        start_kernel,
        in_specs=[SMEM, VMEM, VMEM],
        out_specs=[VMEM] * 4,
        out_shape=[shape(BLOCK, RANK)] * 4,
        compiler_params=params(),
        name="start",
    )(x, buffer, right)


def forward_kernel(x_ref, core_ref, buffer_ref, half_ref, other_ref, *rest):
    *out_refs, gram_ref, both = rest
    core = core_ref[0]
    both[half_of(core, FIRST // 2), :] = half_ref[...]
    both[half_of(1 - core, FIRST // 2), :] = other_ref[...]
    gram_ref[...] = both[COLS:FIRST, :]
    forward_blocks(x_ref[0], buffer_ref, both[0:COLS, :], out_refs)


def forward(x, core, buffer, half, other):
    return pl.pallas_call(
        forward_kernel,
        in_specs=[SMEM, SMEM, VMEM, VMEM, VMEM],
        out_specs=[VMEM] * 5,
        out_shape=[shape(BLOCK, RANK)] * 5,
        scratch_shapes=[scratch(FIRST, RANK)],
        compiler_params=params(),
        name="forward",
    )(x, core, buffer, half, other)


def backward_kernel(x_ref, core_ref, buffer_ref, *rest):
    *left_refs, mine_ref, theirs_ref, left, both = rest
    x, core = x_ref[0], core_ref[0]
    for k in range(4):
        left[tile_of(lax.rem(x + 4 - k, 4)), :] = left_refs[k][...]
    both[0:COLS, :] = dot3(split(buffer_ref[...]), split(left[...]), ((1,), (0,)))
    both[COLS:FIRST, :] = dot(left[...], left[...], ((0,), (0,)))
    mine_ref[...] = both[half_of(core, FIRST // 2), :]
    theirs_ref[...] = both[half_of(1 - core, FIRST // 2), :]


def backward(x, core, buffer, left):
    return pl.pallas_call(
        backward_kernel,
        in_specs=[SMEM, SMEM] + [VMEM] * 5,
        out_specs=[VMEM] * 2,
        out_shape=[shape(FIRST // 2, RANK)] * 2,
        scratch_shapes=[scratch(ROWS, RANK), scratch(FIRST, RANK)],
        compiler_params=params(),
        name="backward",
    )(x, core, buffer, *left)


def prepare_kernel(x_ref, inverse_ref, *rest):
    *left_refs, old_ref = rest
    x = x_ref[0]
    inverse = split(inverse_ref[...])
    for k in range(4):
        place = tile_of(lax.rem(x + 4 - k, 4))
        old_ref[place, :] = dot3(split(left_refs[k][...]), inverse, ((1,), (1,)))


def prepare(x, inverse, left):
    return pl.pallas_call(
        prepare_kernel,
        in_specs=[SMEM] + [VMEM] * 5,
        out_specs=VMEM,
        out_shape=shape(ROWS, RANK),
        cost_estimate=cost(2_000_000_000),
        compiler_params=params(),
        name="prepare",
    )(x, inverse, *left)


def solve_kernel(x_ref, core_ref, buffer_ref, inverse_ref, old_ref, *rest):
    product_refs = rest[0:4]
    mine_ref, theirs_ref, out_ref, carried, gram = rest[4:]
    x, core = x_ref[0], core_ref[0]
    for k in range(4):
        place = tile_of(lax.rem(x + 4 - k, 4))
        out_ref[place, :] = dot(product_refs[k][...], inverse_ref[...], ((1,), (1,)))
    product = out_ref[...]
    carried[...] = dot3(split(buffer_ref[...]), split(product), ((1,), (0,)))
    gram[0:RANK, :] = dot(product, product, ((0,), (0,)))
    gram[RANK:GRAM, :] = jnp.zeros((GRAM - RANK, RANK), jnp.float32)
    gram[RANK : RANK + 1, :] = jnp.sum(old_ref[...] * product, axis=0, keepdims=True)
    for half_ref, position in ((mine_ref, core), (theirs_ref, 1 - core)):
        half_ref[0 : GRAM // 2, :] = gram[half_of(position, GRAM // 2), :]
        half_ref[GRAM // 2 :, :] = carried[half_of(position, COLS // 2), :]


def solve(x, core, buffer, inverse, old, product):
    return pl.pallas_call(
        solve_kernel,
        in_specs=[SMEM, SMEM] + [VMEM] * 7,
        out_specs=[VMEM] * 3,
        out_shape=[shape(GRAM // 2 + COLS // 2, RANK)] * 2 + [shape(ROWS, RANK)],
        scratch_shapes=[scratch(COLS, RANK), scratch(GRAM, RANK)],
        compiler_params=params(),
        name="solve",
    )(x, core, buffer, inverse, old, *product)


def cholesky_inverse(gram_ref, out_ref, block, corner):
    h = RANK // 2
    block[...] = gram_ref[0:h, 0:h]

    def step(k, _):
        inverse = factor(block[...])
        out_ref[half_of(k, h), 0:h] = inverse

        @pl.when(k == 0)
        def _():
            lower = dot(gram_ref[h:, 0:h], inverse, ((1,), (1,)))
            block[...] = gram_ref[h:, h:] - dot(lower, lower, ((1,), (1,)))
            corner[...] = dot(lower, inverse, ((1,), (0,)))

        return 0

    lax.fori_loop(0, 2, step, 0)
    bottom = out_ref[h:, 0:h]
    out_ref[h:, 0:h] = -dot(bottom, corner[...], ((1,), (0,)))
    out_ref[h:, h:] = bottom
    out_ref[0:h, h:] = jnp.zeros((h, h), jnp.float32)


def first_inverse(gram):
    return pl.pallas_call(
        cholesky_inverse,
        in_specs=[VMEM],
        out_specs=VMEM,
        out_shape=shape(RANK, RANK),
        scratch_shapes=[scratch(RANK // 2, RANK // 2)] * 2,
        cost_estimate=cost(10_000_000_000),
        compiler_params=params(),
        name="first_inverse",
    )(gram)


def times_inverse(value, inverse):
    h = RANK // 2
    left = dot(value[:, 0:h], inverse[0:h, 0:h], ((1,), (1,)))
    return jnp.concatenate([left, dot(value, inverse[h:, :], ((1,), (1,)))], 1)


def second_kernel(core_ref, half_ref, other_ref, out_ref, whole, gram, block, corner):
    core = core_ref[0]
    whole[half_of(core, GRAM // 2), :] = half_ref[0 : GRAM // 2, :]
    whole[half_of(1 - core, GRAM // 2), :] = other_ref[0 : GRAM // 2, :]
    scale = 1.0 / jnp.sqrt(jnp.maximum(whole[RANK : RANK + 1, :], 0.0) + EPS)
    gram[...] = (whole[0:RANK, :] * scale).T * scale
    cholesky_inverse(gram, out_ref, block, corner)
    out_ref[...] = out_ref[...] * scale


def second_inverse(core, half, other):
    return pl.pallas_call(
        second_kernel,
        in_specs=[SMEM, VMEM, VMEM],
        out_specs=VMEM,
        out_shape=shape(RANK, RANK),
        scratch_shapes=[scratch(GRAM, RANK), scratch(RANK, RANK)]
        + [scratch(RANK // 2, RANK // 2)] * 2,
        cost_estimate=cost(10_000_000_000),
        compiler_params=params(),
        name="second_inverse",
    )(core, half, other)


def finish_kernel(core_ref, y_ref, inverse_ref, *rest):
    *part_refs, carried_ref, squares_ref, whole = rest
    core, y = core_ref[0], y_ref[0]
    for k in range(4):
        place = lax.rem(y + 4 - k, 4)
        whole[half_of(4 * core + place, PART), :] = part_refs[k][0:PART, :]
        whole[half_of(4 * (1 - core) + place, PART), :] = part_refs[k][PART : 2 * PART, :]
    carried = times_inverse(whole[...], inverse_ref[...])
    carried_ref[...] = carried
    squares = jnp.sum(carried * carried, axis=0, keepdims=True)
    for k in range(32):
        squares_ref[k] = squares


def finish(core, y, inverse, parts):
    return pl.pallas_call(
        finish_kernel,
        in_specs=[SMEM, SMEM] + [VMEM] * 5,
        out_specs=[VMEM] * 2,
        out_shape=[shape(COLS, RANK), shape(32, 1, RANK)],
        scratch_shapes=[scratch(COLS, RANK)],
        compiler_params=params(),
        name="finish",
    )(core, y, inverse, *parts)


def send_columns(out_hbm, staged, semaphores, give):
    wide = ROWS // 2

    def copy(k):
        place = pl.ds(pl.multiple_of(k * wide, wide), wide)
        return pltpu.make_async_copy(staged.at[k], out_hbm.at[:, place], semaphores.at[k])

    def step(k, _):
        staged[k] = give(pl.ds(pl.multiple_of(k * wide, wide), wide))
        copy(k).start()
        return 0

    lax.fori_loop(0, 2, step, 0)
    for k in range(2):
        copy(k).wait()


def feedback_kernel(
    buffer_ref, product_ref, inverse_ref, carried_ref, out_hbm, high_ref, low_ref, *rest
):
    left = times_inverse(product_ref[...], inverse_ref[...])
    high_ref[...], low_ref[...] = split(left)
    carried = split(carried_ref[...])

    def give(place):
        change = dot3(carried, (high_ref[place, :], low_ref[place, :]), ((1,), (1,)))
        return buffer_ref[:, place] - (1.0 - MU) * change

    send_columns(out_hbm, *rest, give)


def feedback(buffer, product, inverse, carried):
    return pl.pallas_call(
        feedback_kernel,
        in_specs=[VMEM] * 4,
        out_specs=[HBM, VMEM, VMEM],
        out_shape=[shape(COLS, ROWS)] + [half_shape(ROWS, RANK)] * 2,
        scratch_shapes=[scratch(2, COLS, ROWS // 2), pltpu.SemaphoreType.DMA((2,))],
        cost_estimate=cost(4_000_000_000),
        compiler_params=params(),
        name="feedback",
    )(buffer, product, inverse, carried)


def update_kernel(high_ref, low_ref, carried_ref, squares_ref, out_hbm, *rest):
    squares = squares_ref[0]
    for k in range(1, 32):
        squares = squares + squares_ref[k]
    right = carried_ref[...] * (((D * FF / RANK) ** 0.5) / jnp.sqrt(squares + EPS))
    right = split(right)

    def give(place):
        return dot3(right, (high_ref[place, :], low_ref[place, :]), ((1,), (1,)))

    send_columns(out_hbm, *rest, give)


def update(high, low, carried, squares):
    return pl.pallas_call(
        update_kernel,
        in_specs=[VMEM] * 4,
        out_specs=HBM,
        out_shape=shape(COLS, ROWS),
        scratch_shapes=[scratch(2, COLS, ROWS // 2), pltpu.SemaphoreType.DMA((2,))],
        compiler_params=params(),
        name="update",
    )(high, low, carried, squares)


def fold_kernel(parts, value_ref, out_ref):
    size = out_ref.shape[0] // parts
    total = value_ref[0:size, :]
    for k in range(1, parts):
        total = total + value_ref[k * size : (k + 1) * size, :]
    for k in range(parts):
        out_ref[k * size : (k + 1) * size, :] = total


def sum_by_exchange(value, axis, groups):
    value = lax.all_to_all(value, axis, 0, 0, tiled=True, axis_index_groups=groups)
    value = pl.pallas_call(
        functools.partial(fold_kernel, len(groups[0])),
        in_specs=[VMEM],
        out_specs=VMEM,
        out_shape=shape(*value.shape),
        compiler_params=params(),
        name="fold",
    )(value)
    return lax.all_to_all(value, axis, 0, 0, tiled=True, axis_index_groups=groups)


def sum_over_col(blocks, beside):
    with jax.named_scope("sum_over_col"):
        total = blocks[0]
        for k in (3, 2, 1):
            total = total + lax.ppermute(blocks[k], "col", X_SHIFTS[k - 1])
        total, beside = lax.optimization_barrier((total, beside))
        total = sum_by_exchange(total, "col", Z_GROUPS)
        rest = [lax.ppermute(total, "col", X_SHIFTS[k - 1]) for k in (1, 2, 3)]
        return [total] + rest, beside


def sum_over_row(mine, theirs):
    with jax.named_scope("sum_over_row"):
        half = mine + lax.ppermute(theirs, "row", OTHER_CORE)
        half = sum_by_exchange(half, "row", Y_GROUPS)
        return half, lax.ppermute(half, "row", OTHER_CORE)


def sum_and_invert(core, y, mine, theirs):
    with jax.named_scope("sum_and_invert"):
        half = mine + lax.ppermute(theirs, "row", OTHER_CORE)
        gram, half = half[: GRAM // 2], half[GRAM // 2 :]

        def share(k):
            part = lax.dynamic_slice_in_dim(half, (y[0] + k) % 4 * PART, PART)
            return jnp.concatenate([gram, part], 0)

        total = share(0)
        for k in (1, 2, 3):
            total = total + lax.ppermute(share(k), "row", Y_SHIFTS[k - 1])
        other = lax.ppermute(total, "row", OTHER_CORE)
        inverse = second_inverse(core, total, other)
        part = jnp.concatenate([total[GRAM // 2 :], other[GRAM // 2 :]], 0)
        parts = [part] + [lax.ppermute(part, "row", shift) for shift in Y_SHIFTS]
        return inverse, *finish(core, y, inverse, parts)


def on_device(momentum, gradient, right_factor):
    x = lax.axis_index("col")[None] % 4
    core = lax.axis_index("row")[None] % 2
    y = lax.axis_index("row")[None] // 2
    buffer = momentum.T + gradient.T
    left, buffer = sum_over_col(start(x, buffer, right_factor), buffer)
    half, other = sum_over_row(*backward(x, core, buffer, left))
    *blocks, gram = forward(x, core, buffer, half, other)
    product, inverse = sum_over_col(blocks, first_inverse(gram))
    old = prepare(x, inverse, left)
    mine, theirs, product = solve(x, core, buffer, inverse, old, product)
    inverse, carried, squares = sum_and_invert(core, y, mine, theirs)
    squares = lax.all_to_all(squares, "col", 0, 0, tiled=True)
    momentum_next, high, low = feedback(buffer, product, inverse, carried)
    return (momentum_next.T, update(high, low, carried, squares).T)


def solution(mesh):
    return jax.shard_map(
        on_device,
        mesh=mesh,
        in_specs=(P("row", "col"), P("row", "col"), P("col", None)),
        out_specs=(P("row", "col"), P("row", "col")),
        check_vma=False,
    )
```
